32 devices in a mesh: wide: 4 (over x, core), narrow: 8 (over z, y).
Axes of the slice: x: 2, y: 2, z: 4, core: 2. Of those that a mesh axis runs over, the one named last changes fastest.
Arguments:
- basis_t: bfloat16 [2048, 64, 256], P(('wide', 'narrow')), may hold values from -0.375 to 0.375
- nested_transfer_matrices: float32 [64, 64, 4096], P(None, None, ('wide', 'narrow')), may hold values from -0.22 to 0.93
- leaf_coupling: float32 [64, 64, 16384], P(None, None, ('wide', 'narrow')), may hold values from -6 to 6
- leaf_columns: int32 [16384], P(('wide', 'narrow')), may hold values from 0 to 2047, as said below
- far_coupling: float32 [64, 64, 512], P(None, None, ('wide', 'narrow')), may hold values from -6 to 6
- far_columns: int32 [512], P(('wide', 'narrow')), may hold values from 0 to 3, as said below
Outputs:
- leaf_coupled: float32 [64, 64, 16384], P(None, None, ('wide', 'narrow'))
- far_coupled: float32 [64, 64, 512], P(None, None, ('wide', 'narrow'))
- group_factors: float32 [32, 64, 64], P(('wide', 'narrow'))
The draws below stay inside these ranges and needn't reach their ends.
Inputs may be any that keep to these rules, and one draw needn't show every extreme that they name: `leaf_columns`: block b's column leaf lies 2 to 64 leaves away from its row leaf b // 8; on every device some block lies exactly 64 leaves away. `far_columns`: block f's column branch differs from its row branch f // 128.
All inputs are finite; a program needn't handle non-finite values.
Results may differ from the reference program's by a relative error of at most 0.0003.
Values sent between devices are 32-bit elements; how exact they have to be, the bound alone decides.
A program may use at most 192 MiB of HBM per device.

```python
import jax
import jax.numpy as jnp
from jax import lax

BASIS_RANK = 64
LEAF_SIZE = 256
LEAF_DEV = 64
NB = 8
BRANCH_COUPLINGS = 16
BRANCHES = 4
GROUP = 8
NLEAF = 2048
NBLK = 16384
NFAR = 512
TRANSFER_SLOTS = 4096


def draw_nested_transfer_matrices(key, part):
    diagonal_jitter = jnp.clip(jax.random.normal(key, (BASIS_RANK, BASIS_RANK, TRANSFER_SLOTS), jnp.float32), -4.0, 4.0) * 0.3
    identity = jnp.eye(BASIS_RANK, dtype=jnp.float32)[:, :, None]
    return (identity + diagonal_jitter * BASIS_RANK ** (-0.5)) * 0.7071


def draw_leaf_columns(key, part):
    block_ids = jnp.arange(NBLK)
    row_leaf = block_ids // NB
    slot_index = block_ids % NB
    position = row_leaf % LEAF_DEV
    distance = jax.random.randint(key, (NBLK,), 2, LEAF_DEV + 1)
    distance = jnp.where((position == 0) & (slot_index == 0), LEAF_DEV, distance)
    distance = jnp.where((position == LEAF_DEV - 1) & (slot_index == 1), LEAF_DEV, distance)
    early_col = row_leaf - distance
    later_col = row_leaf + distance
    column = jnp.where(slot_index % 2 == 0, early_col, later_col)
    column = jnp.where(column < 0, later_col, column)
    column = jnp.where(column >= NLEAF, early_col, column)
    return column.astype(jnp.int32)


def draw_far_columns(key, part):
    block_ids = jnp.arange(NFAR)
    branch = block_ids // (GROUP * BRANCH_COUPLINGS)
    offset = jax.random.randint(key, (NFAR,), 0, BRANCHES - 1)
    return ((branch + 1 + offset) % BRANCHES).astype(jnp.int32)


def block_levels(own_key, extent, cuts, least, top_value):
    loudness, own = 1.0, jax.random.fold_in(own_key, 6)
    for dim, parts in cuts:
        steps = jnp.exp(jax.random.uniform(jax.random.fold_in(own, dim), (parts,), jnp.float32, least / len(cuts), top_value / len(cuts)))
        loudness = loudness * jnp.repeat(steps, extent[dim] // parts).reshape([-1 if axis == dim else 1 for axis in range(len(extent))])
    return loudness


def bell_draw(key, shape, spread, bound, split=(), kind=jnp.bfloat16):
    factor_of = block_levels(key, shape, split, -0.22, 0.18) if split else 1.0
    array = jax.random.normal(key, shape, jnp.float32) * spread * factor_of
    return jnp.minimum(jnp.maximum(array, -bound), bound).astype(kind)


def setup_inputs(seed: int = 0) -> dict:
    splits = jax.random.split(jax.random.key(seed), 7)
    return {
        "basis_t": bell_draw(splits[0], (NLEAF, BASIS_RANK, LEAF_SIZE), LEAF_SIZE ** -0.5, 0.375, ((0, 32),)),
        "nested_transfer_matrices": draw_nested_transfer_matrices(jax.random.fold_in(splits[6], 71), 0),
        "leaf_coupling": bell_draw(splits[2], (BASIS_RANK, BASIS_RANK, NBLK), 1.0, 6.0, ((2, 32),), jnp.float32),
        "leaf_columns": draw_leaf_columns(jax.random.fold_in(splits[6], 71), 0),
        "far_coupling": bell_draw(splits[4], (BASIS_RANK, BASIS_RANK, NFAR), 1.0, 6.0, ((2, 32),), jnp.float32),
        "far_columns": draw_far_columns(jax.random.fold_in(splits[6], 71), 0),
    }


HIGHEST = lax.Precision.HIGHEST

def cholesky_lower(gram_stack):
    full_shape = gram_stack.shape
    rank_size = full_shape[0]
    flat = gram_stack.reshape(rank_size, rank_size, -1)
    row_ids = jnp.arange(rank_size)

    def column_step(column, lower_now):
        row_part = lax.dynamic_index_in_dim(lower_now, column, 0, keepdims=False)
        target = lax.dynamic_index_in_dim(flat, column, 1, keepdims=False) - jnp.einsum('ikb,kb->ib', lower_now, row_part, precision=HIGHEST)
        pivot = jnp.sqrt(lax.dynamic_index_in_dim(target, column, 0, keepdims=False))
        update = jnp.where((row_ids >= column)[:, None], target / pivot[None, :], jnp.zeros_like(target))
        return lax.dynamic_update_index_in_dim(lower_now, update, column, 1)
    result = lax.fori_loop(0, rank_size, column_step, jnp.zeros_like(flat))
    return result.reshape(full_shape)

def join_term(gram_part, transfer_part):
    product = jnp.einsum('kl...,lj...->kj...', gram_part, transfer_part, precision=HIGHEST)
    return jnp.einsum('ki...,kj...->ij...', transfer_part, product, precision=HIGHEST)

def climb_local(gram_leaves, transfer):
    count_now = gram_leaves.shape[-1]
    current = gram_leaves
    while count_now > 1:
        terms_pair = join_term(current, transfer[..., count_now:2 * count_now])
        current = terms_pair[..., 0::2] + terms_pair[..., 1::2]
        count_now = count_now // 2
    return current

def reference(basis_t, nested_transfer_matrices, leaf_coupling, leaf_columns, far_coupling, far_columns):
    basis_wide = basis_t.astype(jnp.float32)
    leaf_gram = jnp.einsum('bkl,bml->kmb', basis_wide, basis_wide, precision=HIGHEST)
    leaf_lower = cholesky_lower(leaf_gram)
    device_count = NLEAF // LEAF_DEV
    transfer_dev = nested_transfer_matrices.reshape(BASIS_RANK, BASIS_RANK, device_count, 2 * LEAF_DEV)
    device_top = climb_local(leaf_gram.reshape(BASIS_RANK, BASIS_RANK, device_count, LEAF_DEV), transfer_dev)[..., 0]
    root_grams = device_top.reshape(BASIS_RANK, BASIS_RANK, BRANCHES, GROUP)
    root_trans = transfer_dev[..., 1].reshape(BASIS_RANK, BASIS_RANK, BRANCHES, GROUP)
    inner_trans = transfer_dev[..., 0].reshape(BASIS_RANK, BASIS_RANK, BRANCHES, GROUP)
    level_list = [root_grams]
    current = root_grams
    count_now = GROUP
    level = 0
    while count_now > 1:
        table = root_trans if level == 0 else inner_trans[..., count_now:2 * count_now]
        terms_pair = join_term(current, table)
        current = terms_pair[..., 0::2] + terms_pair[..., 1::2]
        level_list.append(current)
        count_now = count_now // 2
        level = level + 1
    top_level = len(level_list) - 1
    chosen_list = []
    for narrow_pos in range(GROUP):
        trailing = 0
        while narrow_pos >> trailing & 1 == 1:
            trailing = trailing + 1
        selected_level = trailing + 1
        if selected_level > top_level:
            chosen_list.append(level_list[0][..., narrow_pos])
        else:
            chosen_list.append(level_list[selected_level][..., narrow_pos >> selected_level])
    chosen = jnp.stack(chosen_list, axis=-1)
    group_lower = cholesky_lower(chosen)
    group_factors = jnp.transpose(group_lower, (2, 3, 1, 0)).reshape(device_count, BASIS_RANK, BASIS_RANK)
    branch_lower = cholesky_lower(level_list[top_level][..., 0])
    far_rows = jnp.arange(NFAR) // (GROUP * BRANCH_COUPLINGS)
    row_far_blocks = jnp.take(branch_lower, far_rows.astype(jnp.int32), axis=2)
    col_far = jnp.take(branch_lower, far_columns, axis=2)
    half_far = jnp.einsum('kif,kjf->ijf', row_far_blocks, far_coupling, precision=HIGHEST)
    far_coupled = jnp.einsum('ikf,kjf->ijf', half_far, col_far, precision=HIGHEST)
    blocks_four = leaf_coupling.reshape(BASIS_RANK, BASIS_RANK, NLEAF, NB)
    half_leaf = jnp.einsum('kib,kjbn->ijbn', leaf_lower, blocks_four, precision=HIGHEST)
    col_leaf = jnp.take(leaf_lower, leaf_columns, axis=2).reshape(BASIS_RANK, BASIS_RANK, NLEAF, NB)
    leaf_coupled = jnp.einsum('ikbn,kjbn->ijbn', half_leaf, col_leaf, precision=HIGHEST).reshape(BASIS_RANK, BASIS_RANK, NBLK)
    return (leaf_coupled, far_coupled, group_factors)
```

```python
import functools

import jax
import jax.numpy as jnp
from jax import lax
from jax.experimental import pallas as pl
from jax.experimental.pallas import tpu as pltpu
from jax.sharding import PartitionSpec as P

F32, BF16 = jnp.float32, jnp.bfloat16
VMEM_LIMIT = 56 * 1024 * 1024
NN = (((1,), (0,)), ((), ()))
NT = (((1,), (1,)), ((), ()))


def mm(a, b, dims):
    return lax.dot_general(a, b, dims, preferred_element_type=F32)


def halves(x):
    high = x.astype(BF16)
    return high, (x - high.astype(F32)).astype(BF16)


def mm3(a, b, dims):
    ah, al = halves(a)
    bh, bl = halves(b)
    return mm(ah, bh, dims) + (mm(al, bh, dims) + mm(ah, bl, dims))


def fold(x):
    h = x.shape[0] // 2
    return jnp.concatenate([x[:h], x[h:]], axis=1)


def unfold(x):
    w = x.shape[1] // 2
    return jnp.concatenate([x[:, :w], x[:, w:]], axis=0)


def cholesky_lanes(work, upper, rank):
    lanes = work.shape[2]
    upper[...] = jnp.zeros_like(upper)
    for c0 in range(0, rank, 8):
        left = rank - c0
        if c0 > 0:
            for first in range(c0, c0 + 8, 4):

                def body(e, acc, c0=c0, first=first):
                    v = upper[e, c0:, :]
                    return tuple(
                        acc[r] - upper[e, first + r : first + r + 1, :] * v for r in range(4)
                    )

                acc = tuple(work[first + r, c0:, :] for r in range(4))
                acc = lax.fori_loop(0, c0, body, acc, unroll=4)
                for r in range(4):
                    work[first + r, c0:, :] = acc[r]
        rows = [work[c0 + r, c0:, :] for r in range(8)]
        ids = lax.broadcasted_iota(jnp.int32, (left, lanes), 0)
        for r in range(8):
            pivot = rows[r][r : r + 1]
            v = rows[r] * (1.0 / jnp.sqrt(pivot))
            v = jnp.where(ids >= r, v, 0.0)
            upper[c0 + r, c0:, :] = v
            for later in range(r + 1, 8):
                rows[later] = rows[later] - v[later : later + 1] * v


def leaf_kernel(basis, folded, stage, work, upper):
    leaves, rank = basis.shape[0], basis.shape[1]
    half = rank // 2

    def gram(t, carry):
        b = basis[t]
        stage[pl.ds(t, half, stride=leaves), :] = fold(mm(b, b, NT))
        return carry

    lax.fori_loop(0, leaves, gram, 0, unroll=4)
    for i in range(half):
        turned = stage[i * leaves : (i + 1) * leaves, :].T
        work[i] = turned[:rank]
        work[i + half] = turned[rank:]
    cholesky_lanes(work, upper, rank)
    for i in range(half):
        both = jnp.concatenate([upper[i], upper[i + half]], axis=0)
        stage[i * leaves : (i + 1) * leaves, :] = both.T

    def put(t, carry):
        folded[t] = stage[pl.ds(t, half, stride=leaves), :]
        return carry

    lax.fori_loop(0, leaves, put, 0, unroll=4)


def climb_kernel(basis, transfer, root, message, turned, grams):
    leaves, rank = basis.shape[0], basis.shape[1]
    half = rank // 2
    slots = transfer.shape[1]

    def turn(i, carry):
        both = jnp.concatenate(
            [
                transfer[pl.ds(i, rank, stride=rank), :],
                transfer[pl.ds(i + half, rank, stride=rank), :],
            ],
            axis=0,
        )
        turned[pl.ds(pl.multiple_of(i * slots, slots), slots), :] = both.T
        return carry

    lax.fori_loop(0, half, turn, 0, unroll=4)

    def table(h):
        return unfold(turned[pl.ds(h, half, stride=slots), :])

    def term(g, f):
        return mm3(mm3(f, g, NN), f, NT)

    count = leaves

    def first(p, carry):
        b0, b1 = basis[2 * p], basis[2 * p + 1]
        grams[p] = term(mm(b0, b0, NT), table(count + 2 * p)) + term(
            mm(b1, b1, NT), table(count + 2 * p + 1)
        )
        return carry

    lax.fori_loop(0, count // 2, first, 0, unroll=4)
    count //= 2
    while count > 1:

        def level(p, carry, count=count):
            grams[p] = term(grams[2 * p], table(count + 2 * p)) + term(
                grams[2 * p + 1], table(count + 2 * p + 1)
            )
            return carry

        lax.fori_loop(0, count // 2, level, 0, unroll=min(4, count // 2))
        count //= 2
    root[...] = grams[0]
    message[...] = jnp.concatenate([term(grams[0], table(1)), table(0)], axis=1)


def branch_kernel(slot, gathered, root, group_upper, branch_upper, nodes, stage, work, upper):
    group, rank = gathered.shape[0], gathered.shape[1]
    half = rank // 2
    nodes[0] = root[...]
    count = group
    terms = [gathered[n][:, :rank] for n in range(group)]
    while count > 1:
        count //= 2
        for p in range(count):
            nodes[count + p] = terms[2 * p] + terms[2 * p + 1]
        if count > 1:
            made = []
            for p in range(count):
                f = gathered[count + p][:, rank:]
                made.append(mm3(mm3(f, nodes[count + p], NN), f, NT))
            terms = made
    stage[...] = jnp.ones_like(stage)
    stage[pl.ds(0, half, stride=8), :] = fold(nodes[slot[0]])
    stage[pl.ds(1, half, stride=8), :] = fold(nodes[1])
    for i in range(half):
        turned = stage[i * 8 : (i + 1) * 8, :].T
        work[i] = turned[:rank]
        work[i + half] = turned[rank:]
    cholesky_lanes(work, upper, rank)
    for i in range(half):
        both = jnp.concatenate([upper[i], upper[i + half]], axis=0)
        stage[i * 8 : (i + 1) * 8, :] = both.T
    group_upper[...] = unfold(stage[pl.ds(0, half, stride=8), :])
    branch_upper[...] = stage[pl.ds(1, half, stride=8), :]


def couple_kernel(per_leaf, tables, cols, own, *refs):
    x, out, ready, turned, mid, done = refs[tables:]
    half = own.shape[1]
    rank = 2 * half
    slab = x.shape[1]
    step = pl.program_id(0)

    @pl.when(step == 0)
    def _():
        for place, ref in enumerate(refs[:tables]):
            leaves = ref.shape[0]

            def prepare(t, carry, first=place * leaves, ref=ref):
                hi, lo = halves(unfold(ref[t]))
                ready[first + t] = jnp.concatenate([hi, hi, lo], axis=1)
                return carry

            lax.fori_loop(0, leaves, prepare, 0, unroll=4)

    def turn(j, carry):
        both = jnp.concatenate(
            [x[pl.ds(j, rank, stride=rank), :], x[pl.ds(j + half, rank, stride=rank), :]], axis=0
        )
        turned[j] = both.T
        return carry

    lax.fori_loop(0, half, turn, 0, unroll=4)
    here = slab // per_leaf

    def leaf(t, carry):
        rows = turned[:, pl.ds(pl.multiple_of(t * per_leaf, per_leaf), per_leaf), :]
        a = rows.reshape(half * per_leaf, 2 * rank)
        ah, al = halves(a)
        u = unfold(own[step * here + t])
        zero = jnp.zeros_like(u)
        wide = jnp.concatenate(
            [jnp.concatenate([u, zero], axis=1), jnp.concatenate([zero, u], axis=1)], axis=0
        )
        wh, wl = halves(wide)
        mid[...] = mm(
            jnp.concatenate([ah, al], axis=1), jnp.concatenate([wh, wh], axis=1), NT
        ) + mm(ah, wl, NT)
        for n in range(per_leaf):
            h = unfold(mid[pl.ds(n, half, stride=per_leaf), :])
            hh, hl = halves(h)
            s = cols[step * slab + t * per_leaf + n]
            made = mm(ready[s], jnp.concatenate([hh, hl, hh], axis=0), NN)
            done[pl.ds(t * per_leaf + n, half, stride=slab), :] = fold(made)
        return carry

    lax.fori_loop(0, here, leaf, 0, unroll=2)

    def turn_back(l, carry):
        back = done[pl.ds(pl.multiple_of(l * slab, slab), slab), :].T
        out[pl.ds(l, rank, stride=rank), :] = back[:rank]
        out[pl.ds(l + half, rank, stride=rank), :] = back[rank:]
        return carry

    lax.fori_loop(0, half, turn_back, 0, unroll=4)


def vmem():
    return pl.BlockSpec(memory_space=pltpu.VMEM)


def smem():
    return pl.BlockSpec(memory_space=pltpu.SMEM)


def params():
    return pltpu.CompilerParams(vmem_limit_bytes=VMEM_LIMIT)


def leaf_factors(basis_t):
    leaves, rank = basis_t.shape[:2]
    half = rank // 2
    return pl.pallas_call(
        leaf_kernel,
        out_shape=jax.ShapeDtypeStruct((leaves, half, 2 * rank), F32),
        in_specs=[vmem()],
        out_specs=vmem(),
        scratch_shapes=[
            pltpu.VMEM((half * leaves, 2 * rank), F32),
            pltpu.VMEM((rank, rank, leaves), F32),
            pltpu.VMEM((rank, rank, leaves), F32),
        ],
        compiler_params=params(),
        name="leaf_factors",
    )(basis_t)


def climb(basis_t, transfer):
    leaves, rank = basis_t.shape[:2]
    slots = transfer.shape[2]
    return pl.pallas_call(
        climb_kernel,
        out_shape=(
            jax.ShapeDtypeStruct((rank, rank), F32),
            jax.ShapeDtypeStruct((rank, 2 * rank), F32),
        ),
        in_specs=[vmem(), vmem()],
        out_specs=(vmem(), vmem()),
        scratch_shapes=[
            pltpu.VMEM((rank // 2 * slots, 2 * rank), F32),
            pltpu.VMEM((leaves // 2, rank, rank), F32),
        ],
        compiler_params=params(),
        name="climb",
    )(basis_t, transfer.reshape(rank * rank, slots))


def branch(slot, gathered, root):
    group, rank = gathered.shape[:2]
    return pl.pallas_call(
        branch_kernel,
        out_shape=(
            jax.ShapeDtypeStruct((rank, rank), F32),
            jax.ShapeDtypeStruct((rank // 2, 2 * rank), F32),
        ),
        in_specs=[smem(), vmem(), vmem()],
        out_specs=(vmem(), vmem()),
        scratch_shapes=[
            pltpu.VMEM((group, rank, rank), F32),
            pltpu.VMEM((rank // 2 * 8, 2 * rank), F32),
            pltpu.VMEM((rank, rank, 8), F32),
            pltpu.VMEM((rank, rank, 8), F32),
        ],
        compiler_params=params(),
        name="branch",
    )(slot, gathered, root)


def couple(cols, own, tables, coupling):
    leaves, half = own.shape[:2]
    kept = tables[0].shape[0]
    rank = 2 * half
    blocks = coupling.shape[2]
    slab = min(128, blocks)
    per_leaf = blocks // leaves
    out = pl.pallas_call(
        functools.partial(couple_kernel, per_leaf, len(tables)),
        out_shape=jax.ShapeDtypeStruct((rank * rank, blocks), F32),
        grid=(blocks // slab,),
        in_specs=[
            smem(),
            *[pl.BlockSpec(f.shape, lambda g: (0, 0, 0)) for f in (own, *tables)],
            pl.BlockSpec((rank * rank, slab), lambda g: (0, g)),
        ],
        out_specs=pl.BlockSpec((rank * rank, slab), lambda g: (0, g)),
        scratch_shapes=[
            pltpu.VMEM((len(tables) * kept, rank, 3 * rank), BF16),
            pltpu.VMEM((half, slab, 2 * rank), F32),
            pltpu.VMEM((half * per_leaf, 2 * rank), F32),
            pltpu.VMEM((half * slab, 2 * rank), F32),
        ],
        compiler_params=params(),
        name="couple",
    )(cols, own, *tables, coupling.reshape(rank * rank, blocks))
    return out.reshape(rank, rank, blocks)


def on_device(
    basis_t, nested_transfer_matrices, leaf_coupling, leaf_columns, far_coupling, far_columns
):
    leaves = basis_t.shape[0]
    both = ("wide", "narrow")
    devices = lax.axis_size(both)
    first_leaf = lax.axis_index(both) * leaves - leaves
    own = leaf_factors(basis_t)
    before = lax.ppermute(own, both, [(i, i + 1) for i in range(devices - 1)])
    after = lax.ppermute(own, both, [(i + 1, i) for i in range(devices - 1)])
    root, message = climb(basis_t, nested_transfer_matrices)
    gathered = lax.all_gather(message, "narrow", axis=0)
    leaf_coupled = couple(leaf_columns - first_leaf, own, (before, own, after), leaf_coupling)

    group = lax.axis_size("narrow")
    depth = group.bit_length() - 1
    n = lax.axis_index("narrow")
    slot = jnp.zeros((), jnp.int32)
    for level in range(1, depth + 1):
        slot = jnp.where(n % 2**level == 2 ** (level - 1) - 1, (group + n) >> level, slot)
    group_upper, branch_upper = branch(slot.reshape(1).astype(jnp.int32), gathered, root)
    branch_all = lax.all_gather(branch_upper, "wide", axis=0)
    far_coupled = couple(far_columns, branch_upper[None], (branch_all,), far_coupling)
    return (leaf_coupled, far_coupled, group_upper[None])


def solution(mesh):
    in_specs = (
        P(("wide", "narrow"), None, None),
        P(None, None, ("wide", "narrow")),
        P(None, None, ("wide", "narrow")),
        P(("wide", "narrow")),
        P(None, None, ("wide", "narrow")),
        P(("wide", "narrow")),
    )
    out_specs = (
        P(None, None, ("wide", "narrow")),
        P(None, None, ("wide", "narrow")),
        P(("wide", "narrow"), None, None),
    )
    return jax.shard_map(
        on_device, mesh=mesh, in_specs=in_specs, out_specs=out_specs, check_vma=False
    )
```

```python
import functools

import jax
import jax.numpy as jnp
from jax import lax
from jax.experimental import pallas as pl
from jax.experimental.pallas import tpu as pltpu
from jax.sharding import PartitionSpec as P

F32, BF16 = jnp.float32, jnp.bfloat16
VMEM_LIMIT = 56 * 1024 * 1024
NN = (((1,), (0,)), ((), ()))
NT = (((1,), (1,)), ((), ()))


def mm(a, b, dims):
    return lax.dot_general(a, b, dims, preferred_element_type=F32)


def halves(x):
    high = x.astype(BF16)
    return high, (x - high.astype(F32)).astype(BF16)


def mm3(a, b, dims):
    ah, al = halves(a)
    bh, bl = halves(b)
    return mm(ah, bh, dims) + (mm(al, bh, dims) + mm(ah, bl, dims))


def fold(x):
    h = x.shape[0] // 2
    return jnp.concatenate([x[:h], x[h:]], axis=1)


def unfold(x):
    w = x.shape[1] // 2
    return jnp.concatenate([x[:, :w], x[:, w:]], axis=0)


def cholesky_lanes(work, upper, rank):
    lanes = work.shape[2]
    upper[...] = jnp.zeros_like(upper)
    for c0 in range(0, rank, 8):
        left = rank - c0
        if c0 > 0:
            for first in range(c0, c0 + 8, 4):

                def body(e, acc, c0=c0, first=first):
                    v = upper[e, c0:, :]
                    return tuple(
                        acc[r] - upper[e, first + r : first + r + 1, :] * v for r in range(4)
                    )

                acc = tuple(work[first + r, c0:, :] for r in range(4))
                acc = lax.fori_loop(0, c0, body, acc, unroll=4)
                for r in range(4):
                    work[first + r, c0:, :] = acc[r]
        rows = [work[c0 + r, c0:, :] for r in range(8)]
        ids = lax.broadcasted_iota(jnp.int32, (left, lanes), 0)
        for r in range(8):
            pivot = rows[r][r : r + 1]
            v = rows[r] * (1.0 / jnp.sqrt(pivot))
            v = jnp.where(ids >= r, v, 0.0)
            upper[c0 + r, c0:, :] = v
            for later in range(r + 1, 8):
                rows[later] = rows[later] - v[later : later + 1] * v


def leaf_kernel(basis, folded, stage, work, upper):
    leaves, rank = basis.shape[0], basis.shape[1]
    half = rank // 2

    def gram(t, carry):
        b = basis[t]
        stage[pl.ds(t, half, stride=leaves), :] = fold(mm(b, b, NT))
        return carry

    lax.fori_loop(0, leaves, gram, 0, unroll=4)
    for i in range(half):
        turned = stage[i * leaves : (i + 1) * leaves, :].T
        work[i] = turned[:rank]
        work[i + half] = turned[rank:]
    cholesky_lanes(work, upper, rank)
    for i in range(half):
        both = jnp.concatenate([upper[i], upper[i + half]], axis=0)
        stage[i * leaves : (i + 1) * leaves, :] = both.T

    def put(t, carry):
        folded[t] = stage[pl.ds(t, half, stride=leaves), :]
        return carry

    lax.fori_loop(0, leaves, put, 0, unroll=4)


def climb_kernel(basis, transfer, root, message, turned, grams):
    leaves, rank = basis.shape[0], basis.shape[1]
    half = rank // 2
    slots = transfer.shape[1]

    def turn(i, carry):
        both = jnp.concatenate(
            [
                transfer[pl.ds(i, rank, stride=rank), :],
                transfer[pl.ds(i + half, rank, stride=rank), :],
            ],
            axis=0,
        )
        turned[pl.ds(pl.multiple_of(i * slots, slots), slots), :] = both.T
        return carry

    lax.fori_loop(0, half, turn, 0, unroll=4)

    def table(h):
        return unfold(turned[pl.ds(h, half, stride=slots), :])

    def term(g, f):
        return mm3(mm3(f, g, NN), f, NT)

    count = leaves

    def first(p, carry):
        b0, b1 = basis[2 * p], basis[2 * p + 1]
        grams[p] = term(mm(b0, b0, NT), table(count + 2 * p)) + term(
            mm(b1, b1, NT), table(count + 2 * p + 1)
        )
        return carry

    lax.fori_loop(0, count // 2, first, 0, unroll=16)
    count //= 2
    while count > 1:

        def level(p, carry, count=count):
            grams[p] = term(grams[2 * p], table(count + 2 * p)) + term(
                grams[2 * p + 1], table(count + 2 * p + 1)
            )
            return carry

        lax.fori_loop(0, count // 2, level, 0, unroll=min(16, count // 2))
        count //= 2
    root[...] = grams[0]
    message[...] = jnp.concatenate([term(grams[0], table(1)), table(0)], axis=1)


def branch_kernel(slot, gathered, root, group_upper, branch_upper, nodes, stage, work, upper):
    group, rank = gathered.shape[0], gathered.shape[1]
    half = rank // 2
    nodes[0] = root[...]
    count = group
    terms = [gathered[n][:, :rank] for n in range(group)]
    while count > 1:
        count //= 2
        for p in range(count):
            nodes[count + p] = terms[2 * p] + terms[2 * p + 1]
        if count > 1:
            made = []
            for p in range(count):
                f = gathered[count + p][:, rank:]
                made.append(mm3(mm3(f, nodes[count + p], NN), f, NT))
            terms = made
    stage[...] = jnp.ones_like(stage)
    stage[pl.ds(0, half, stride=8), :] = fold(nodes[slot[0]])
    stage[pl.ds(1, half, stride=8), :] = fold(nodes[1])
    for i in range(half):
        turned = stage[i * 8 : (i + 1) * 8, :].T
        work[i] = turned[:rank]
        work[i + half] = turned[rank:]
    cholesky_lanes(work, upper, rank)
    for i in range(half):
        both = jnp.concatenate([upper[i], upper[i + half]], axis=0)
        stage[i * 8 : (i + 1) * 8, :] = both.T
    group_upper[...] = unfold(stage[pl.ds(0, half, stride=8), :])
    branch_upper[...] = stage[pl.ds(1, half, stride=8), :]


def couple_kernel(per_leaf, tables, cols, own, *refs):
    x, out, ready, turned, mid, done = refs[tables:]
    half = own.shape[1]
    rank = 2 * half
    slab = x.shape[1]
    step = pl.program_id(0)

    @pl.when(step == 0)
    def _():
        for place, ref in enumerate(refs[:tables]):
            leaves = ref.shape[0]

            def prepare(t, carry, first=place * leaves, ref=ref):
                hi, lo = halves(unfold(ref[t]))
                ready[first + t] = jnp.concatenate([hi, hi, lo], axis=1)
                return carry

            lax.fori_loop(0, leaves, prepare, 0, unroll=4)

    def turn(j, carry):
        both = jnp.concatenate(
            [x[pl.ds(j, rank, stride=rank), :], x[pl.ds(j + half, rank, stride=rank), :]], axis=0
        )
        turned[j] = both.T
        return carry

    lax.fori_loop(0, half, turn, 0, unroll=4)
    here = slab // per_leaf

    together = mid.shape[0]

    def some(first, carry):
        for m in range(together):
            t = first * together + m
            rows = turned[:, pl.ds(pl.multiple_of(t * per_leaf, per_leaf), per_leaf), :]
            ah, al = halves(rows.reshape(half * per_leaf, 2 * rank))
            u = unfold(own[step * here + t])
            zero = jnp.zeros_like(u)
            wide = jnp.concatenate(
                [jnp.concatenate([u, zero], axis=1), jnp.concatenate([zero, u], axis=1)], axis=0
            )
            wh, wl = halves(wide)
            mid[m] = mm(
                jnp.concatenate([ah, al], axis=1), jnp.concatenate([wh, wh], axis=1), NT
            ) + mm(ah, wl, NT)
        for m in range(together):
            for n in range(per_leaf):
                b = (first * together + m) * per_leaf + n
                hh, hl = halves(unfold(mid[m, pl.ds(n, half, stride=per_leaf), :]))
                s = cols[step * slab + b]
                made = mm(ready[s], jnp.concatenate([hh, hl, hh], axis=0), NN)
                done[pl.ds(b, half, stride=slab), :] = fold(made)
        return carry

    lax.fori_loop(0, here // together, some, 0)

    def turn_back(l, carry):
        back = done[pl.ds(pl.multiple_of(l * slab, slab), slab), :].T
        out[pl.ds(l, rank, stride=rank), :] = back[:rank]
        out[pl.ds(l + half, rank, stride=rank), :] = back[rank:]
        return carry

    lax.fori_loop(0, half, turn_back, 0, unroll=4)


def spread_kernel(axis, x, out, send, recv, local):
    count = out.shape[0]
    me = lax.axis_index(axis)
    barrier = pltpu.get_barrier_semaphore()
    for k in range(1, count):
        pl.semaphore_signal(
            barrier,
            inc=1,
            device_id={axis: lax.rem(me + k, count)},
            device_id_type=pl.DeviceIdType.MESH,
        )
    pl.semaphore_wait(barrier, count - 1)
    copies = [pltpu.make_async_copy(x, out.at[me], local)]
    for k in range(1, count):
        copies.append(
            pltpu.make_async_remote_copy(
                src_ref=x,
                dst_ref=out.at[me],
                send_sem=send.at[k - 1],
                recv_sem=recv.at[k - 1],
                device_id={axis: lax.rem(me + k, count)},
                device_id_type=pl.DeviceIdType.MESH,
            )
        )
    for copy in copies:
        copy.start()
    for copy in copies:
        copy.wait()


def spread(x, axis, collective_id):
    count = lax.axis_size(axis)
    return pl.pallas_call(
        functools.partial(spread_kernel, axis),
        out_shape=jax.ShapeDtypeStruct((count,) + x.shape, x.dtype),
        in_specs=[vmem()],
        out_specs=vmem(),
        scratch_shapes=[
            pltpu.SemaphoreType.DMA((count - 1,)),
            pltpu.SemaphoreType.DMA((count - 1,)),
            pltpu.SemaphoreType.DMA,
        ],
        compiler_params=pltpu.CompilerParams(collective_id=collective_id, has_side_effects=True),
        name="spread_" + axis,
    )(x)


def vmem():
    return pl.BlockSpec(memory_space=pltpu.VMEM)


def smem():
    return pl.BlockSpec(memory_space=pltpu.SMEM)


def params():
    return pltpu.CompilerParams(vmem_limit_bytes=VMEM_LIMIT)


def leaf_factors(basis_t):
    leaves, rank = basis_t.shape[:2]
    half = rank // 2
    return pl.pallas_call(
        leaf_kernel,
        out_shape=jax.ShapeDtypeStruct((leaves, half, 2 * rank), F32),
        in_specs=[vmem()],
        out_specs=vmem(),
        scratch_shapes=[
            pltpu.VMEM((half * leaves, 2 * rank), F32),
            pltpu.VMEM((rank, rank, leaves), F32),
            pltpu.VMEM((rank, rank, leaves), F32),
        ],
        compiler_params=params(),
        name="leaf_factors",
    )(basis_t)


def climb(basis_t, transfer):
    leaves, rank = basis_t.shape[:2]
    slots = transfer.shape[2]
    return pl.pallas_call(
        climb_kernel,
        out_shape=(
            jax.ShapeDtypeStruct((rank, rank), F32),
            jax.ShapeDtypeStruct((rank, 2 * rank), F32),
        ),
        in_specs=[vmem(), vmem()],
        out_specs=(vmem(), vmem()),
        scratch_shapes=[
            pltpu.VMEM((rank // 2 * slots, 2 * rank), F32),
            pltpu.VMEM((leaves // 2, rank, rank), F32),
        ],
        compiler_params=params(),
        name="climb",
    )(basis_t, transfer.reshape(rank * rank, slots))


def branch(slot, gathered, root):
    group, rank = gathered.shape[:2]
    return pl.pallas_call(
        branch_kernel,
        out_shape=(
            jax.ShapeDtypeStruct((rank, rank), F32),
            jax.ShapeDtypeStruct((rank // 2, 2 * rank), F32),
        ),
        in_specs=[smem(), vmem(), vmem()],
        out_specs=(vmem(), vmem()),
        scratch_shapes=[
            pltpu.VMEM((group, rank, rank), F32),
            pltpu.VMEM((rank // 2 * 8, 2 * rank), F32),
            pltpu.VMEM((rank, rank, 8), F32),
            pltpu.VMEM((rank, rank, 8), F32),
        ],
        compiler_params=params(),
        name="branch",
    )(slot, gathered, root)


def couple(cols, own, tables, coupling):
    leaves, half = own.shape[:2]
    kept = tables[0].shape[0]
    rank = 2 * half
    blocks = coupling.shape[2]
    slab = min(128, blocks)
    per_leaf = blocks // leaves
    together = min(4, slab // per_leaf)
    out = pl.pallas_call(
        functools.partial(couple_kernel, per_leaf, len(tables)),
        out_shape=jax.ShapeDtypeStruct((rank * rank, blocks), F32),
        grid=(blocks // slab,),
        in_specs=[
            smem(),
            *[pl.BlockSpec(f.shape, lambda g: (0, 0, 0)) for f in (own, *tables)],
            pl.BlockSpec((rank * rank, slab), lambda g: (0, g)),
        ],
        out_specs=pl.BlockSpec((rank * rank, slab), lambda g: (0, g)),
        scratch_shapes=[
            pltpu.VMEM((len(tables) * kept, rank, 3 * rank), BF16),
            pltpu.VMEM((half, slab, 2 * rank), F32),
            pltpu.VMEM((together, half * per_leaf, 2 * rank), F32),
            pltpu.VMEM((half * slab, 2 * rank), F32),
        ],
        compiler_params=params(),
        name="couple",
    )(cols, own, *tables, coupling.reshape(rank * rank, blocks))
    return out.reshape(rank, rank, blocks)


def on_device(
    basis_t, nested_transfer_matrices, leaf_coupling, leaf_columns, far_coupling, far_columns
):
    leaves = basis_t.shape[0]
    both = ("wide", "narrow")
    devices = lax.axis_size(both)
    first_leaf = lax.axis_index(both) * leaves - leaves
    own = leaf_factors(basis_t)
    before = lax.ppermute(own, both, [(i, i + 1) for i in range(devices - 1)])
    after = lax.ppermute(own, both, [(i + 1, i) for i in range(devices - 1)])
    root, message = climb(basis_t, nested_transfer_matrices)
    gathered = spread(message, "narrow", 0)
    leaf_coupled = couple(leaf_columns - first_leaf, own, (before, own, after), leaf_coupling)

    group = lax.axis_size("narrow")
    depth = group.bit_length() - 1
    n = lax.axis_index("narrow")
    slot = jnp.zeros((), jnp.int32)
    for level in range(1, depth + 1):
        slot = jnp.where(n % 2**level == 2 ** (level - 1) - 1, (group + n) >> level, slot)
    group_upper, branch_upper = branch(slot.reshape(1).astype(jnp.int32), gathered, root)
    branch_all = spread(branch_upper, "wide", 1)
    far_coupled = couple(far_columns, branch_upper[None], (branch_all,), far_coupling)
    return (leaf_coupled, far_coupled, group_upper[None])


def solution(mesh):
    in_specs = (
        P(("wide", "narrow"), None, None),
        P(None, None, ("wide", "narrow")),
        P(None, None, ("wide", "narrow")),
        P(("wide", "narrow")),
        P(None, None, ("wide", "narrow")),
        P(("wide", "narrow")),
    )
    out_specs = (
        P(None, None, ("wide", "narrow")),
        P(None, None, ("wide", "narrow")),
        P(("wide", "narrow"), None, None),
    )
    return jax.shard_map(
        on_device, mesh=mesh, in_specs=in_specs, out_specs=out_specs, check_vma=False
    )
```
